32 devices in a mesh: tgt: 4 (over z), src: 8 (over y, x, core).
Axes of the slice: x: 2, y: 2, z: 4, core: 2. Of those that a mesh axis runs over, the one named last changes fastest.
Arguments:
- target_xy: float32 [2, 2048], P(None, 'tgt'), may hold values from 0 to 20
- source_xy: float32 [2, 16384], P(None, 'src'), may hold values from 0 to 20
- body_of: int32 [16384], P('src'), may hold values from 0 to 127
- series_coef: float32 [2, 32, 128], replicated, may hold values from -2 to 2
- probe_matrix: bfloat16 [16384, 128], P('src'), may hold values from -0.046875 to 0.046875
- row_weight: float32 [2048], P('tgt'), may hold values from 1 to 36
Outputs:
- basis: float32 [2048, 256], P(('tgt', 'src'))
- factor: float32 [128, 128], replicated
The draws below stay inside these ranges and needn't reach their ends.
All inputs are finite; a program needn't handle non-finite values.
Results may differ from the reference program's by a relative error of at most 0.0085.
Values sent between devices are 32-bit elements; how exact they have to be, the bound alone decides.
A program may use at most 64 MiB of HBM per device.

```python
import jax
import jax.numpy as jnp
from jax import lax

T_DEV = 512
S_DEV = 2048
K = 128
NTERMS = 32
BODIES = 128
TARGETS = 2048
SOURCES = 16384
N_TGT = 4
N_SRC = 8


def draw_row_weight(key, part):
    spread = jax.random.uniform(key, (TARGETS,), jnp.float32)
    place = jnp.arange(TARGETS).astype(jnp.float32) / TARGETS
    return jnp.exp(jnp.log(4.0) * spread) * jnp.exp(jnp.log(3.0) * place)


def place_ends(array, rng, low, top_value):
    spot = [jax.random.randint(jax.random.fold_in(rng, axis), (), 0, length) for axis, length in enumerate(array.shape)]
    main_axis = array.shape.index(max(array.shape))
    beside = spot[:main_axis] + [(spot[main_axis] + 1) % array.shape[main_axis]] + spot[main_axis + 1:]
    return array.at[tuple(spot)].set(low).at[tuple(beside)].set(top_value)


def levels(key, extent, cuts, low, top_value):
    def one(axis_at, shards_of):
        steps = jax.random.uniform(jax.random.fold_in(jax.random.fold_in(key, 6), axis_at), (shards_of,), jnp.float32, low / len(cuts), top_value / len(cuts))
        return jnp.repeat(jnp.exp(steps), extent[axis_at] // shards_of).reshape((-1,) + (1,) * (len(extent) - axis_at - 1))

    gain = one(*cuts[0])
    for cut in cuts[1:]:
        gain = gain * one(*cut)
    return gain


def bell_draw(stream_key, shape, width, bound, shards=(), kind=jnp.bfloat16):
    entries = width * jax.random.normal(stream_key, shape, jnp.float32)
    if shards:
        entries = entries * levels(stream_key, shape, shards, -0.22, 0.18)
    return jnp.clip(entries, -bound, bound).astype(kind)


def setup_inputs(seed: int = 0) -> dict:
    streams_of = jax.random.split(jax.random.key(seed), 7)
    target_xy = jnp.clip(20.0 * jax.random.uniform(streams_of[0], (2, TARGETS), jnp.float32) ** levels(streams_of[0], (2, TARGETS), ((1, 4),), -0.2, 0.2), 0.0, 20.0)
    source_xy = jnp.clip(20.0 * jax.random.uniform(streams_of[1], (2, SOURCES), jnp.float32) ** levels(streams_of[1], (2, SOURCES), ((1, 8),), -0.2, 0.2), 0.0, 20.0)
    body_of = place_ends(jax.random.randint(streams_of[2], (SOURCES,), 0, BODIES), jax.random.fold_in(streams_of[2], 1), 0, BODIES - 1).astype(jnp.int32)
    series_coef = bell_draw(streams_of[3], (2, NTERMS, BODIES), 0.3, 2.0, (), jnp.float32)
    probe_matrix = bell_draw(streams_of[4], (SOURCES, K), SOURCES ** -0.5, 0.046875, ((0, 8),))
    row_weight = draw_row_weight(jax.random.fold_in(streams_of[6], 71), 0)
    return dict(target_xy=target_xy, source_xy=source_xy, body_of=body_of, series_coef=series_coef, probe_matrix=probe_matrix, row_weight=row_weight)


def panel_series(rows_xy, cols_xy, coef_re, coef_im):
    delta_x = rows_xy[0][:, None] - cols_xy[0][None, :]
    delta_y = rows_xy[1][:, None] - cols_xy[1][None, :]
    radius = jnp.sqrt(delta_x * delta_x + delta_y * delta_y + 0.25)
    decay_rate = jnp.exp(-0.005 * radius)
    step_re = decay_rate * jnp.cos(1.5 * radius)
    step_im = decay_rate * jnp.sin(1.5 * radius)
    term_count = coef_re.shape[0]
    total_re = jnp.broadcast_to(coef_re[term_count - 1][None, :], radius.shape)
    total_im = jnp.broadcast_to(coef_im[term_count - 1][None, :], radius.shape)
    for degree in range(term_count - 2, -1, -1):
        next_re = total_re * step_re - total_im * step_im + coef_re[degree][None, :]
        next_im = total_re * step_im + total_im * step_re + coef_im[degree][None, :]
        total_re, total_im = (next_re, next_im)
    series_re = total_re * step_re - total_im * step_im
    series_im = total_re * step_im + total_im * step_re
    tile_re = (1.0 / radius + series_re).astype(jnp.bfloat16)
    tile_im = series_im.astype(jnp.bfloat16)
    return (tile_re, tile_im)

def reference(target_xy, source_xy, body_of, series_coef, probe_matrix, row_weight):
    picked = series_coef[:, :, body_of]
    src_xy = source_xy.reshape(2, N_SRC, S_DEV).transpose(1, 0, 2)
    src_coef = picked.reshape(2, NTERMS, N_SRC, S_DEV).transpose(2, 0, 1, 3)
    src_probe = probe_matrix.reshape(N_SRC, S_DEV, K)

    def one_rows(rows_xy):

        def add_block(totals, pieces):
            xy_block, coef_block, probe_block = pieces
            tile_re, tile_im = panel_series(rows_xy, xy_block, coef_block[0], coef_block[1])
            part_re = jnp.dot(tile_re.astype(jnp.float32), probe_block.astype(jnp.float32), preferred_element_type=jnp.float32)
            part_im = jnp.dot(tile_im.astype(jnp.float32), probe_block.astype(jnp.float32), preferred_element_type=jnp.float32)
            return (totals + jnp.concatenate([part_re, part_im], axis=1), None)
        start_totals = jnp.zeros((rows_xy.shape[1], 2 * K), jnp.float32)
        totals, _ = lax.scan(add_block, start_totals, (src_xy, src_coef, src_probe))
        return totals
    tgt_blocks = target_xy.reshape(2, N_TGT, T_DEV).transpose(1, 0, 2)
    sketch = lax.map(one_rows, tgt_blocks).reshape(TARGETS, 2 * K)
    weighted = sketch * row_weight[:, None]
    stacked = weighted.reshape(2 * TARGETS, K)
    gram = jnp.dot(stacked.T, stacked, precision=lax.Precision.HIGHEST) / (2.0 * TARGETS)
    lower_factor = jnp.linalg.cholesky(gram)
    identity = jnp.eye(K, dtype=jnp.float32)
    inverse = lax.linalg.triangular_solve(lower_factor, identity, left_side=True, lower=True)
    basis = jnp.dot(stacked, inverse.T, precision=lax.Precision.HIGHEST).reshape(TARGETS, 2 * K)
    return (basis, lower_factor.T)
```

```python
import functools
import math

import jax
import jax.numpy as jnp
from jax import lax
from jax.experimental import pallas as pl
from jax.experimental.pallas import tpu as pltpu
from jax.sharding import PartitionSpec as P

LANES = 128
TURNS = 1.5 / (2.0 * math.pi)
ROUNDER = 12582912.0
SIN_TERMS = (1.570796322, -0.6459634782, 0.07968022286, -0.004602163105)
COS_TERMS = (0.9999999724, -1.233697011, 0.2535986077, -0.02040825547)


def horner(terms, point):
    total = terms[-1]
    for term in terms[-2::-1]:
        total = total * point + term
    return total


def wave_step(tx, ty, sx, sy):
    delta_x = tx - sx
    delta_y = ty - sy
    squared = delta_x * delta_x + delta_y * delta_y + 0.25
    inverse = lax.rsqrt(squared)
    radius = squared * inverse
    radius = radius + (0.5 * inverse) * (squared - radius * radius)
    turns = radius * TURNS
    part = turns - ((turns + ROUNDER) - ROUNDER)
    point = part * part
    sine = horner(SIN_TERMS, point) * part
    cosine = horner(COS_TERMS, point)
    for _ in range(2):
        sine, cosine = 2.0 * sine * cosine, 1.0 - 2.0 * sine * sine
    decay = jnp.exp(-0.005 * radius)
    return inverse, decay * cosine, decay * sine


def spread_rows(row):
    return jnp.transpose(jnp.broadcast_to(row, (LANES, LANES)))


def pick_coefficients(coef, bodies):
    count = coef.shape[1]
    one_hot = (
        lax.broadcasted_iota(jnp.int32, (count, bodies.shape[1]), 0) == bodies
    ).astype(jnp.float32).astype(jnp.bfloat16)
    picked = None
    rest = coef
    for _ in range(3):
        part = rest.astype(jnp.bfloat16)
        rest = rest - part.astype(jnp.float32)
        term = jnp.dot(part, one_hot, preferred_element_type=jnp.float32)
        picked = term if picked is None else picked + term
    return picked


def sketch_kernel(row_block, width, txy, sxy, body, coef, probe, out, spread, picked):
    rows = txy.shape[1]
    sources = sxy.shape[1]
    terms = coef.shape[0] // 2
    blocks = sources // width
    for axis in range(2):
        for start in range(0, rows, LANES):
            spread[axis, start : start + LANES, :] = spread_rows(
                txy[axis : axis + 1, start : start + LANES]
            )

    def pick(block, carry):
        at = pl.ds(pl.multiple_of(block * width, width), width)
        picked[:, at] = pick_coefficients(coef[...], body[:, at])
        return carry

    lax.fori_loop(0, blocks, pick, 0)

    def half(row_at, start):
        at = pl.ds(pl.multiple_of(start, LANES), LANES)
        inverse, step_re, step_im = wave_step(
            spread[0, row_at, :], spread[1, row_at, :], sxy[0:1, at], sxy[1:2, at]
        )

        def term(index):
            return picked[index : index + 1, at]

        total_re, total_im = term(terms - 1), term(2 * terms - 1)
        for degree in range(terms - 2, -1, -1):
            total_re, total_im = (
                (total_re * step_re - total_im * step_im) + term(degree),
                (total_re * step_im + total_im * step_re) + term(terms + degree),
            )
        series_re = total_re * step_re - total_im * step_im
        series_im = total_re * step_im + total_im * step_re
        return (inverse + series_re).astype(jnp.bfloat16), series_im.astype(jnp.bfloat16)

    def tile(row_at, block):
        halves = [half(row_at, block * width + start) for start in range(0, width, LANES)]
        return jnp.concatenate(
            [jnp.concatenate([h[0] for h in halves], axis=1),
             jnp.concatenate([h[1] for h in halves], axis=1)], axis=0)

    def product(held, block):
        at = pl.ds(pl.multiple_of(block * width, width), width)
        return jnp.dot(held, probe[at, :], preferred_element_type=jnp.float32)

    def chunk(index, carry):
        row_at = pl.ds(pl.multiple_of(index * row_block, row_block), row_block)

        def step(block, state):
            held, total = state
            total = total + product(held, block - 1)
            return tile(row_at, block), total

        zero = jnp.zeros((2 * row_block, LANES), jnp.float32)
        held, total = lax.fori_loop(1, blocks, step, (tile(row_at, 0), zero))
        total = total + product(held, blocks - 1)
        out[row_at, :LANES] = total[:row_block]
        out[row_at, LANES:] = total[row_block:]
        return carry

    lax.fori_loop(0, rows // row_block, chunk, 0)


def sketch(target_xy, source_xy, body_of, series_coef, probe_matrix):
    rows = target_xy.shape[1]
    sources = source_xy.shape[1]
    table = series_coef.reshape(-1, series_coef.shape[2])
    return pl.pallas_call(
        functools.partial(sketch_kernel, math.gcd(rows, 64), 2 * LANES),
        out_shape=jax.ShapeDtypeStruct((rows, 2 * probe_matrix.shape[1]), jnp.float32),
        in_specs=[pl.BlockSpec(memory_space=pltpu.VMEM)] * 5,
        out_specs=pl.BlockSpec(memory_space=pltpu.VMEM),
        scratch_shapes=[
            pltpu.VMEM((2, rows, LANES), jnp.float32),
            pltpu.VMEM((table.shape[0], sources), jnp.float32),
        ],
        compiler_params=pltpu.CompilerParams(vmem_limit_bytes=32 * 1024 * 1024),
        name="sketch",
    )(target_xy, source_xy, body_of[None, :], table, probe_matrix)


def per_device(target_xy, source_xy, body_of, series_coef, probe_matrix, row_weight):
    rank_width = probe_matrix.shape[1]
    rows_all = target_xy.shape[1]
    own_count = rows_all // lax.axis_size("src")
    scale_rows = float(2 * rows_all * lax.axis_size("tgt"))
    own_start = lax.axis_index("src") * own_count
    partial_value = sketch(target_xy, source_xy, body_of, series_coef, probe_matrix)
    own_rows = lax.psum_scatter(partial_value, "src", scatter_dimension=0, tiled=True)
    own_weight = lax.dynamic_slice_in_dim(row_weight, own_start, own_count, 0)
    stacked = (own_rows * own_weight[:, None]).reshape(-1, rank_width)
    gram = jnp.dot(stacked.T, stacked, precision=lax.Precision.HIGHEST)
    gram = lax.psum(gram, ("tgt", "src")) / scale_rows
    lower_factor = jnp.linalg.cholesky(gram)
    identity = jnp.eye(rank_width, dtype=jnp.float32)
    inverse = lax.linalg.triangular_solve(lower_factor, identity, left_side=True, lower=True)
    basis_rows = jnp.dot(stacked, inverse.T, precision=lax.Precision.HIGHEST)
    return (basis_rows.reshape(own_count, 2 * rank_width), lower_factor.T)


def solution(mesh):
    return jax.shard_map(
        per_device,
        mesh=mesh,
        in_specs=(P(None, "tgt"), P(None, "src"), P("src"), P(), P("src", None), P("tgt")),
        out_specs=(P(("tgt", "src"), None), P()),
        check_vma=False,
    )
```

```python
import functools
import math

import jax
import jax.numpy as jnp
from jax import lax
from jax.experimental import pallas as pl
from jax.experimental.pallas import tpu as pltpu
from jax.sharding import PartitionSpec as P

LANES = 128
TURNS = 1.5 / (2.0 * math.pi)
ROUNDER = 12582912.0
SIN_TERMS = (1.570796322, -0.6459634782, 0.07968022286, -0.004602163105)
COS_TERMS = (0.9999999724, -1.233697011, 0.2535986077, -0.02040825547)


def horner(terms, point):
    total = terms[-1]
    for term in terms[-2::-1]:
        total = total * point + term
    return total


def wave_step(tx, ty, sx, sy):
    delta_x = tx - sx
    delta_y = ty - sy
    squared = delta_x * delta_x + delta_y * delta_y + 0.25
    inverse = lax.rsqrt(squared)
    radius = squared * inverse
    radius = radius + (0.5 * inverse) * (squared - radius * radius)
    turns = radius * TURNS
    part = turns - ((turns + ROUNDER) - ROUNDER)
    point = part * part
    sine = horner(SIN_TERMS, point) * part
    cosine = horner(COS_TERMS, point)
    for _ in range(2):
        sine, cosine = 2.0 * sine * cosine, 1.0 - 2.0 * sine * sine
    decay = jnp.exp(-0.005 * radius)
    return inverse, decay * cosine, decay * sine


def spread_rows(row):
    return jnp.transpose(jnp.broadcast_to(row, (LANES, LANES)))


def pick_coefficients(coef, bodies):
    count = coef.shape[1]
    one_hot = (
        lax.broadcasted_iota(jnp.int32, (count, bodies.shape[1]), 0) == bodies
    ).astype(jnp.float32).astype(jnp.bfloat16)
    picked = None
    rest = coef
    for _ in range(3):
        part = rest.astype(jnp.bfloat16)
        rest = rest - part.astype(jnp.float32)
        term = jnp.dot(part, one_hot, preferred_element_type=jnp.float32)
        picked = term if picked is None else picked + term
    return picked


def remote(source, target, send_sem, recv_sem, axis, peer):
    return pltpu.make_async_remote_copy(
        src_ref=source,
        dst_ref=target,
        send_sem=send_sem,
        recv_sem=recv_sem,
        device_id={axis: peer},
        device_id_type=pl.DeviceIdType.MESH,
    )


def guarded(condition, needed, action):
    if needed:
        pl.when(condition)(action)
    else:
        action()


def sketch_kernel(
    row_block, width, n_src, n_tgt, scale,
    txy_in, sxy_in, body_in, coef_in, probe_in, weight_in, stacked_out, gram_out,
    txy, sxy, body, coef, probe, weight, spread, picked, sums, landed,
    gram_mine, gram_landed, piece_mine, piece_landed, gram_full,
    in_sem, row_send, row_recv, gram_send, gram_recv, tgt_send, tgt_recv, all_send, all_recv,
):
    src_me = lax.axis_index("src")
    tgt_me = lax.axis_index("tgt")
    src_peers = [lax.rem(src_me + offset, n_src) for offset in range(1, n_src)]
    tgt_peers = [lax.rem(tgt_me + offset, n_tgt) for offset in range(1, n_tgt)]
    barrier = pltpu.get_barrier_semaphore()
    for axis, peers in (("src", src_peers), ("tgt", tgt_peers)):
        for peer in peers:
            pl.semaphore_signal(
                barrier, inc=1, device_id={axis: peer}, device_id_type=pl.DeviceIdType.MESH
            )

    loads = [
        pltpu.make_async_copy(start, end, in_sem.at[index])
        for index, (start, end) in enumerate(
            ((txy_in, txy), (sxy_in, sxy), (body_in, body), (coef_in, coef),
             (weight_in, weight), (probe_in, probe))
        )
    ]
    for load in loads:
        load.start()
    for load in loads:
        load.wait()

    rows = txy.shape[1]
    sources = sxy.shape[1]
    terms = coef.shape[0] // 2
    blocks = sources // width
    own = rows // n_src
    chunks = rows // row_block
    owners_in = row_block // own
    rank_width = probe.shape[1]
    piece = piece_mine.shape[0]
    owners = rank_width // piece

    for axis in range(3):
        for start in range(0, rows, LANES):
            at = slice(start, start + LANES)
            row = weight[0:1, at] if axis == 2 else txy[axis : axis + 1, at]
            spread[axis, at, :] = spread_rows(row)

    def pick(block, carry):
        at = pl.ds(pl.multiple_of(block * width, width), width)
        picked[:, at] = pick_coefficients(coef[...], body[:, at])
        return carry

    lax.fori_loop(0, blocks, pick, 0)

    def half(row_at, start):
        at = pl.ds(pl.multiple_of(start, LANES), LANES)
        inverse, step_re, step_im = wave_step(
            spread[0, row_at, :], spread[1, row_at, :], sxy[0:1, at], sxy[1:2, at]
        )

        def term(index):
            return picked[index : index + 1, at]

        total_re, total_im = term(terms - 1), term(2 * terms - 1)
        for degree in range(terms - 2, -1, -1):
            total_re, total_im = (
                (total_re * step_re - total_im * step_im) + term(degree),
                (total_re * step_im + total_im * step_re) + term(terms + degree),
            )
        series_re = total_re * step_re - total_im * step_im
        series_im = total_re * step_im + total_im * step_re
        return (inverse + series_re).astype(jnp.bfloat16), series_im.astype(jnp.bfloat16)

    def tile(row_at, block):
        halves = [half(row_at, block * width + start) for start in range(0, width, LANES)]
        return jnp.concatenate(
            [jnp.concatenate([h[0] for h in halves], axis=1),
             jnp.concatenate([h[1] for h in halves], axis=1)], axis=0)

    def product(held, block):
        at = pl.ds(pl.multiple_of(block * width, width), width)
        return jnp.dot(held, probe[at, :], preferred_element_type=jnp.float32)

    def owned(owner):
        return sums.at[pl.ds(pl.multiple_of(owner * own, own), own), :]

    def chunk(turn, carry):
        index = lax.rem(turn + 1 + src_me // owners_in, chunks)
        row_at = pl.ds(pl.multiple_of(index * row_block, row_block), row_block)

        def step(block, state):
            held, total = state
            total = total + product(held, block - 1)
            return tile(row_at, block), total

        zero = jnp.zeros((2 * row_block, LANES), jnp.float32)
        held, total = lax.fori_loop(1, blocks, step, (tile(row_at, 0), zero))
        total = total + product(held, blocks - 1)
        sums[row_at, :LANES] = total[:row_block]
        sums[row_at, LANES:] = total[row_block:]

        @pl.when(turn == 0)
        def _():
            pl.semaphore_wait(barrier, len(src_peers) + len(tgt_peers))

        for inner in range(owners_in):
            owner = index * owners_in + inner

            @pl.when(owner != src_me)
            def _():
                remote(owned(owner), landed.at[src_me], row_send.at[owner], row_recv.at[src_me],
                       "src", owner).start()

        return carry

    lax.fori_loop(0, chunks, chunk, 0)

    own_at = pl.ds(pl.multiple_of(src_me * own, own), own)
    landed[src_me] = sums[own_at, :]
    for peer in src_peers:
        remote(owned(peer), landed.at[peer], row_send.at[peer], row_recv.at[peer],
               "src", peer).wait()
    total = landed[0]
    for sender in range(1, n_src):
        total = total + landed[sender]
    own_weight = spread[2, own_at, :]
    stacked = jnp.concatenate(
        [total[:, :rank_width] * own_weight, total[:, rank_width:] * own_weight], axis=0)
    stacked_out[...] = stacked
    gram_mine[...] = lax.dot_general(
        stacked, stacked, (((0,), (0,)), ((), ())),
        precision=lax.Precision.HIGHEST, preferred_element_type=jnp.float32)

    def part_of(ref, owner):
        return ref.at[pl.ds(pl.multiple_of(owner * piece, piece), piece), :]

    some_idle = owners < n_src
    mine = src_me < owners
    for peer in src_peers:
        guarded(peer < owners, some_idle, lambda peer=peer: remote(
            part_of(gram_mine, peer), gram_landed.at[src_me], gram_send.at[peer],
            gram_recv.at[src_me], "src", peer).start())

    def merge():
        at = pl.ds(pl.multiple_of(src_me * piece, piece), piece)
        gram_landed[src_me] = gram_mine[at, :]
        for peer in src_peers:
            remote(part_of(gram_mine, src_me), gram_landed.at[peer], gram_send.at[peer],
                   gram_recv.at[peer], "src", peer).wait_recv()
        merged = gram_landed[0]
        for sender in range(1, n_src):
            merged = merged + gram_landed[sender]
        piece_mine[...] = merged
        copies = [remote(piece_mine, piece_landed.at[tgt_me], tgt_send.at[peer],
                         tgt_recv.at[tgt_me], "tgt", peer) for peer in tgt_peers]
        for copy in copies:
            copy.start()
        piece_landed[tgt_me] = merged
        for peer in tgt_peers:
            remote(piece_mine, piece_landed.at[peer], tgt_send.at[peer],
                   tgt_recv.at[peer], "tgt", peer).wait_recv()
        whole = piece_landed[0]
        for sender in range(1, n_tgt):
            whole = whole + piece_landed[sender]
        gram_full[at, :] = whole * scale
        sends = [remote(part_of(gram_full, src_me), part_of(gram_full, src_me),
                        all_send.at[peer], all_recv.at[src_me], "src", peer)
                 for peer in src_peers]
        for copy in sends:
            copy.start()
        for copy in copies + sends:
            copy.wait_send()

    guarded(mine, some_idle, merge)
    for peer in src_peers:
        guarded(peer < owners, some_idle, lambda peer=peer: remote(
            part_of(gram_mine, peer), part_of(gram_full, peer), gram_send.at[peer],
            all_recv.at[peer], "src", peer).wait())
    gram_out[...] = gram_full[...]


def sketch(target_xy, source_xy, body_of, series_coef, probe_matrix, row_weight):
    rows = target_xy.shape[1]
    sources, rank_width = probe_matrix.shape
    n_src = lax.axis_size("src")
    n_tgt = lax.axis_size("tgt")
    own = rows // n_src
    table = series_coef.reshape(-1, series_coef.shape[2])
    inputs = (target_xy, source_xy, body_of[None, :], table, probe_matrix, row_weight[None, :])
    piece = max(8, rank_width // n_src)
    dma = pltpu.SemaphoreType.DMA
    held = [pltpu.VMEM(inputs[i].shape, inputs[i].dtype) for i in range(6)]
    scale = 1.0 / (2.0 * rows * n_tgt)
    return pl.pallas_call(
        functools.partial(sketch_kernel, max(own, math.gcd(rows, 64)), 2 * LANES, n_src, n_tgt, scale),
        out_shape=(
            jax.ShapeDtypeStruct((2 * own, rank_width), jnp.float32),
            jax.ShapeDtypeStruct((rank_width, rank_width), jnp.float32),
        ),
        in_specs=[pl.BlockSpec(memory_space=pl.ANY)] * 6,
        out_specs=[pl.BlockSpec(memory_space=pltpu.VMEM)] * 2,
        scratch_shapes=held + [
            pltpu.VMEM((3, rows, LANES), jnp.float32),
            pltpu.VMEM((table.shape[0], sources), jnp.float32),
            pltpu.VMEM((rows, 2 * rank_width), jnp.float32),
            pltpu.VMEM((n_src, own, 2 * rank_width), jnp.float32),
            pltpu.VMEM((rank_width, rank_width), jnp.float32),
            pltpu.VMEM((n_src, piece, rank_width), jnp.float32),
            pltpu.VMEM((piece, rank_width), jnp.float32),
            pltpu.VMEM((n_tgt, piece, rank_width), jnp.float32),
            pltpu.VMEM((rank_width, rank_width), jnp.float32),
            dma((6,)), dma((n_src,)), dma((n_src,)), dma((n_src,)), dma((n_src,)),
            dma((n_tgt,)), dma((n_tgt,)), dma((n_src,)), dma((n_src,)),
        ],
        compiler_params=pltpu.CompilerParams(
            collective_id=0, has_side_effects=True, vmem_limit_bytes=60 * 1024 * 1024
        ),
        name="sketch",
    )(*inputs)


def factor_kernel(own, stacked, gram, basis, factor, work, inverse):
    size = gram.shape[0]
    rows_at = lax.broadcasted_iota(jnp.int32, (size, size), 0)
    columns_at = lax.broadcasted_iota(jnp.int32, (size, size), 1)
    work[:, :size] = gram[...]
    work[:, size:] = jnp.where(rows_at == columns_at, 1.0, 0.0)
    depth = 8
    sub = lax.broadcasted_iota(jnp.int32, (depth, size), 0)

    def row_of(block, index):
        return jnp.broadcast_to(block[index : index + 1, :], (depth, size))

    for start in range(0, size, depth):
        end = start + depth
        left = work[start:end, :size]
        right = work[start:end, size:]
        columns = [
            jnp.broadcast_to(left[:, start + c : start + c + 1], (depth, size))
            for c in range(depth)
        ]
        pivots = None
        for k in range(depth):
            pivot = row_of(columns[k], k)
            pivots = pivot if pivots is None else jnp.where(sub >= k, pivot, pivots)
            if k == depth - 1:
                break
            ratio = jnp.where(sub > k, columns[k] / pivot, 0.0)
            for c in range(k + 1, depth):
                columns[c] = columns[c] - ratio * row_of(columns[c], k)
            left = left - ratio * row_of(left, k)
            right = right - ratio * row_of(right, k)
        gain = 1.0 / jnp.sqrt(pivots)
        left = left * gain
        right = right * gain
        left = jnp.where(columns_at[:depth] >= start + sub, left, 0.0)
        factor[start:end, :] = left
        inverse[start:end, :] = right
        if end < size:
            both = jnp.concatenate([left, right], axis=1)
            work[end:, :] = work[end:, :] - lax.dot_general(
                left[:, end:], both, (((0,), (0,)), ((), ())),
                precision=lax.Precision.HIGHEST, preferred_element_type=jnp.float32)
    result = lax.dot_general(
        stacked[...], inverse[...], (((1,), (1,)), ((), ())),
        precision=lax.Precision.HIGHEST, preferred_element_type=jnp.float32)
    basis[:, :size] = result[:own]
    basis[:, size:] = result[own:]


def orthonormalize(stacked, gram):
    size = gram.shape[0]
    own = stacked.shape[0] // 2
    return pl.pallas_call(
        functools.partial(factor_kernel, own),
        out_shape=(
            jax.ShapeDtypeStruct((own, 2 * size), jnp.float32),
            jax.ShapeDtypeStruct((size, size), jnp.float32),
        ),
        in_specs=[pl.BlockSpec(memory_space=pltpu.VMEM)] * 2,
        out_specs=[pl.BlockSpec(memory_space=pltpu.VMEM)] * 2,
        scratch_shapes=[
            pltpu.VMEM((size, 2 * size), jnp.float32),
            pltpu.VMEM((size, size), jnp.float32),
        ],
        name="orthonormalize",
    )(stacked, gram)


def per_device(*arguments):
    return orthonormalize(*sketch(*arguments))


def solution(mesh):
    return jax.shard_map(
        per_device,
        mesh=mesh,
        in_specs=(P(None, "tgt"), P(None, "src"), P("src"), P(), P("src", None), P("tgt")),
        out_specs=(P(("tgt", "src"), None), P()),
        check_vma=False,
    )
```

```python
import functools
import math

import jax
import jax.numpy as jnp
from jax import lax
from jax.experimental import pallas as pl
from jax.experimental.pallas import tpu as pltpu
from jax.sharding import PartitionSpec as P

LANES = 128
TURNS = 1.5 / (2.0 * math.pi)
ROUNDER = 12582912.0
SIN_TERMS = (1.570796322, -0.6459634782, 0.07968022286, -0.004602163105)
COS_TERMS = (0.9999999724, -1.233697011, 0.2535986077, -0.02040825547)


def horner(terms, point):
    total = terms[-1]
    for term in terms[-2::-1]:
        total = total * point + term
    return total


def wave_step(tx, ty, sx, sy):
    delta_x = tx - sx
    delta_y = ty - sy
    squared = delta_x * delta_x + delta_y * delta_y + 0.25
    inverse = lax.rsqrt(squared)
    radius = squared * inverse
    radius = radius + (0.5 * inverse) * (squared - radius * radius)
    turns = radius * TURNS
    part = turns - ((turns + ROUNDER) - ROUNDER)
    point = part * part
    sine = horner(SIN_TERMS, point) * part
    cosine = horner(COS_TERMS, point)
    for _ in range(2):
        doubled = sine + sine
        sine, cosine = doubled * cosine, 1.0 - doubled * sine
    decay = jnp.exp2((-0.005 * math.log2(math.e)) * radius)
    return inverse, decay * cosine, decay * sine


def spread_rows(row):
    return jnp.transpose(jnp.broadcast_to(row, (LANES, LANES)))


def pick_coefficients(coef, bodies):
    count = coef.shape[1]
    one_hot = (
        lax.broadcasted_iota(jnp.int32, (count, bodies.shape[1]), 0) == bodies
    ).astype(jnp.float32).astype(jnp.bfloat16)
    picked = None
    rest = coef
    for _ in range(3):
        part = rest.astype(jnp.bfloat16)
        rest = rest - part.astype(jnp.float32)
        term = jnp.dot(part, one_hot, preferred_element_type=jnp.float32)
        picked = term if picked is None else picked + term
    return picked


def remote(source, target, send_sem, recv_sem, axis, peer):
    return pltpu.make_async_remote_copy(
        src_ref=source,
        dst_ref=target,
        send_sem=send_sem,
        recv_sem=recv_sem,
        device_id={axis: peer},
        device_id_type=pl.DeviceIdType.MESH,
    )


def guarded(condition, needed, action):
    if needed:
        pl.when(condition)(action)
    else:
        action()


def sketch_kernel(
    row_block, width, n_src, n_tgt, scale,
    txy_in, sxy_in, body_in, coef_in, probe_in, weight_in, stacked_out, gram_out,
    txy, sxy, body, coef, probe, weight, spread, picked, sums, landed,
    gram_mine, gram_landed, piece_mine, piece_landed, gram_full,
    in_sem, row_send, row_recv, gram_send, gram_recv, tgt_send, tgt_recv, all_send, all_recv,
):
    src_me = lax.axis_index("src")
    tgt_me = lax.axis_index("tgt")
    src_peers = [lax.rem(src_me + offset, n_src) for offset in range(1, n_src)]
    tgt_peers = [lax.rem(tgt_me + offset, n_tgt) for offset in range(1, n_tgt)]
    barrier = pltpu.get_barrier_semaphore()
    for axis, peers in (("src", src_peers), ("tgt", tgt_peers)):
        for peer in peers:
            pl.semaphore_signal(
                barrier, inc=1, device_id={axis: peer}, device_id_type=pl.DeviceIdType.MESH
            )

    loads = [
        pltpu.make_async_copy(start, end, in_sem.at[index])
        for index, (start, end) in enumerate(
            ((txy_in, txy), (sxy_in, sxy), (body_in, body), (coef_in, coef),
             (weight_in, weight), (probe_in, probe))
        )
    ]
    for load in loads:
        load.start()
    for load in loads:
        load.wait()

    rows = txy.shape[1]
    sources = sxy.shape[1]
    terms = coef.shape[0] // 2
    blocks = sources // width
    own = rows // n_src
    chunks = rows // row_block
    owners_in = row_block // own
    rank_width = probe.shape[1]
    piece = piece_mine.shape[0]
    owners = rank_width // piece

    for axis in range(3):
        for start in range(0, rows, LANES):
            at = slice(start, start + LANES)
            row = weight[0:1, at] if axis == 2 else txy[axis : axis + 1, at]
            spread[axis, at, :] = spread_rows(row)

    def pick(block, carry):
        at = pl.ds(pl.multiple_of(block * width, width), width)
        picked[:, at] = pick_coefficients(coef[...], body[:, at])
        return carry

    lax.fori_loop(0, blocks, pick, 0, unroll=True)

    def half(row_at, start):
        at = pl.ds(pl.multiple_of(start, LANES), LANES)
        inverse, step_re, step_im = wave_step(
            spread[0, row_at, :], spread[1, row_at, :], sxy[0:1, at], sxy[1:2, at]
        )

        def term(index):
            return picked[index : index + 1, at]

        total_re, total_im = term(terms - 1), term(2 * terms - 1)
        for degree in range(terms - 2, -1, -1):
            total_re, total_im = (
                (total_re * step_re - total_im * step_im) + term(degree),
                (total_re * step_im + total_im * step_re) + term(terms + degree),
            )
        series_re = total_re * step_re - total_im * step_im
        series_im = total_re * step_im + total_im * step_re
        return (inverse + series_re).astype(jnp.bfloat16), series_im.astype(jnp.bfloat16)

    def tile(row_at, block):
        halves = [half(row_at, block * width + start) for start in range(0, width, LANES)]
        return jnp.concatenate(
            [jnp.concatenate([h[0] for h in halves], axis=1),
             jnp.concatenate([h[1] for h in halves], axis=1)], axis=0)

    def product(held, block):
        at = pl.ds(pl.multiple_of(block * width, width), width)
        return jnp.dot(held, probe[at, :], preferred_element_type=jnp.float32)

    def owned(owner):
        return sums.at[pl.ds(pl.multiple_of(owner * own, own), own), :]

    def chunk(turn, carry):
        index = lax.rem(turn + 1 + src_me // owners_in, chunks)
        row_at = pl.ds(pl.multiple_of(index * row_block, row_block), row_block)

        def step(block, state):
            held, total = state
            total = total + product(held, block - 1)
            return tile(row_at, block), total

        zero = jnp.zeros((2 * row_block, LANES), jnp.float32)
        held, total = lax.fori_loop(1, blocks, step, (tile(row_at, 0), zero))
        total = total + product(held, blocks - 1)
        sums[row_at, :LANES] = total[:row_block]
        sums[row_at, LANES:] = total[row_block:]

        @pl.when(turn == 0)
        def _():
            pl.semaphore_wait(barrier, len(src_peers) + len(tgt_peers))

        for inner in range(owners_in):
            owner = index * owners_in + inner

            @pl.when(owner != src_me)
            def _():
                remote(owned(owner), landed.at[src_me], row_send.at[owner], row_recv.at[src_me],
                       "src", owner).start()

        return carry

    lax.fori_loop(0, chunks, chunk, 0)

    own_at = pl.ds(pl.multiple_of(src_me * own, own), own)
    landed[src_me] = sums[own_at, :]
    for peer in src_peers:
        remote(owned(peer), landed.at[peer], row_send.at[peer], row_recv.at[peer],
               "src", peer).wait()
    total = landed[0]
    for sender in range(1, n_src):
        total = total + landed[sender]
    own_weight = spread[2, own_at, :]
    stacked = jnp.concatenate(
        [total[:, :rank_width] * own_weight, total[:, rank_width:] * own_weight], axis=0)
    stacked_out[...] = stacked
    gram_mine[...] = lax.dot_general(
        stacked, stacked, (((0,), (0,)), ((), ())),
        precision=lax.Precision.HIGHEST, preferred_element_type=jnp.float32)

    def part_of(ref, owner):
        return ref.at[pl.ds(pl.multiple_of(owner * piece, piece), piece), :]

    some_idle = owners < n_src
    mine = src_me < owners
    for peer in src_peers:
        guarded(peer < owners, some_idle, lambda peer=peer: remote(
            part_of(gram_mine, peer), gram_landed.at[src_me], gram_send.at[peer],
            gram_recv.at[src_me], "src", peer).start())

    def merge():
        at = pl.ds(pl.multiple_of(src_me * piece, piece), piece)
        gram_landed[src_me] = gram_mine[at, :]
        for peer in src_peers:
            remote(part_of(gram_mine, src_me), gram_landed.at[peer], gram_send.at[peer],
                   gram_recv.at[peer], "src", peer).wait_recv()
        merged = gram_landed[0]
        for sender in range(1, n_src):
            merged = merged + gram_landed[sender]
        piece_mine[...] = merged
        copies = [remote(piece_mine, piece_landed.at[tgt_me], tgt_send.at[peer],
                         tgt_recv.at[tgt_me], "tgt", peer) for peer in tgt_peers]
        for copy in copies:
            copy.start()
        piece_landed[tgt_me] = merged
        for peer in tgt_peers:
            remote(piece_mine, piece_landed.at[peer], tgt_send.at[peer],
                   tgt_recv.at[peer], "tgt", peer).wait_recv()
        whole = piece_landed[0]
        for sender in range(1, n_tgt):
            whole = whole + piece_landed[sender]
        gram_full[at, :] = whole * scale
        sends = [remote(part_of(gram_full, src_me), part_of(gram_full, src_me),
                        all_send.at[peer], all_recv.at[src_me], "src", peer)
                 for peer in src_peers]
        for copy in sends:
            copy.start()
        for copy in copies + sends:
            copy.wait_send()

    guarded(mine, some_idle, merge)
    for peer in src_peers:
        guarded(peer < owners, some_idle, lambda peer=peer: remote(
            part_of(gram_mine, peer), part_of(gram_full, peer), gram_send.at[peer],
            all_recv.at[peer], "src", peer).wait())
    gram_out[...] = gram_full[...]


def sketch(target_xy, source_xy, body_of, series_coef, probe_matrix, row_weight):
    rows = target_xy.shape[1]
    sources, rank_width = probe_matrix.shape
    n_src = lax.axis_size("src")
    n_tgt = lax.axis_size("tgt")
    own = rows // n_src
    table = series_coef.reshape(-1, series_coef.shape[2])
    inputs = (target_xy, source_xy, body_of[None, :], table, probe_matrix, row_weight[None, :])
    piece = max(8, rank_width // n_src)
    dma = pltpu.SemaphoreType.DMA
    held = [pltpu.VMEM(inputs[i].shape, inputs[i].dtype) for i in range(6)]
    scale = 1.0 / (2.0 * rows * n_tgt)
    return pl.pallas_call(
        functools.partial(sketch_kernel, max(own, math.gcd(rows, 64)), 4 * LANES, n_src, n_tgt, scale),
        out_shape=(
            jax.ShapeDtypeStruct((2 * own, rank_width), jnp.float32),
            jax.ShapeDtypeStruct((rank_width, rank_width), jnp.float32),
        ),
        in_specs=[pl.BlockSpec(memory_space=pl.ANY)] * 6,
        out_specs=[pl.BlockSpec(memory_space=pltpu.VMEM)] * 2,
        scratch_shapes=held + [
            pltpu.VMEM((3, rows, LANES), jnp.float32),
            pltpu.VMEM((table.shape[0], sources), jnp.float32),
            pltpu.VMEM((rows, 2 * rank_width), jnp.float32),
            pltpu.VMEM((n_src, own, 2 * rank_width), jnp.float32),
            pltpu.VMEM((rank_width, rank_width), jnp.float32),
            pltpu.VMEM((n_src, piece, rank_width), jnp.float32),
            pltpu.VMEM((piece, rank_width), jnp.float32),
            pltpu.VMEM((n_tgt, piece, rank_width), jnp.float32),
            pltpu.VMEM((rank_width, rank_width), jnp.float32),
            dma((6,)), dma((n_src,)), dma((n_src,)), dma((n_src,)), dma((n_src,)),
            dma((n_tgt,)), dma((n_tgt,)), dma((n_src,)), dma((n_src,)),
        ],
        compiler_params=pltpu.CompilerParams(
            collective_id=0, has_side_effects=True, vmem_limit_bytes=60 * 1024 * 1024
        ),
        name="sketch",
    )(*inputs)


def factor_kernel(own, stacked, gram, basis, factor, work, inverse):
    size = gram.shape[0]
    rows_at = lax.broadcasted_iota(jnp.int32, (size, size), 0)
    columns_at = lax.broadcasted_iota(jnp.int32, (size, size), 1)
    work[:, :size] = gram[...]
    work[:, size:] = jnp.where(rows_at == columns_at, 1.0, 0.0)
    depth = 32
    sub = lax.broadcasted_iota(jnp.int32, (depth, size), 0)

    def row_of(block, index):
        return jnp.broadcast_to(block[index : index + 1, :], (depth, size))

    for start in range(0, size, depth):
        end = start + depth
        left = work[start:end, :size]
        right = work[start:end, size:]
        columns = [
            jnp.broadcast_to(left[:, start + c : start + c + 1], (depth, size))
            for c in range(depth)
        ]
        pivots = None
        for k in range(depth):
            pivot = row_of(columns[k], k)
            pivots = pivot if pivots is None else jnp.where(sub >= k, pivot, pivots)
            if k == depth - 1:
                break
            ratio = jnp.where(sub > k, columns[k], 0.0) * (1.0 / pivot)
            for c in range(k + 1, depth):
                columns[c] = columns[c] - ratio * row_of(columns[c], k)
            left = left - ratio * row_of(left, k)
            right = right - ratio * row_of(right, k)
        gain = 1.0 / jnp.sqrt(pivots)
        left = left * gain
        right = right * gain
        left = jnp.where(columns_at[:depth] >= start + sub, left, 0.0)
        factor[start:end, :] = left
        inverse[start:end, :] = right
        if end < size:
            both = jnp.concatenate([left, right], axis=1)
            work[end:, :] = work[end:, :] - lax.dot_general(
                left[:, end:], both, (((0,), (0,)), ((), ())),
                precision=lax.Precision.HIGHEST, preferred_element_type=jnp.float32)
    result = lax.dot_general(
        stacked[...], inverse[...], (((1,), (1,)), ((), ())),
        precision=lax.Precision.HIGHEST, preferred_element_type=jnp.float32)
    basis[:, :size] = result[:own]
    basis[:, size:] = result[own:]


def orthonormalize(stacked, gram):
    size = gram.shape[0]
    own = stacked.shape[0] // 2
    return pl.pallas_call(
        functools.partial(factor_kernel, own),
        out_shape=(
            jax.ShapeDtypeStruct((own, 2 * size), jnp.float32),
            jax.ShapeDtypeStruct((size, size), jnp.float32),
        ),
        in_specs=[pl.BlockSpec(memory_space=pltpu.VMEM)] * 2,
        out_specs=[pl.BlockSpec(memory_space=pltpu.VMEM)] * 2,
        scratch_shapes=[
            pltpu.VMEM((size, 2 * size), jnp.float32),
            pltpu.VMEM((size, size), jnp.float32),
        ],
        name="orthonormalize",
    )(stacked, gram)


def per_device(*arguments):
    return orthonormalize(*sketch(*arguments))


def solution(mesh):
    return jax.shard_map(
        per_device,
        mesh=mesh,
        in_specs=(P(None, "tgt"), P(None, "src"), P("src"), P(), P("src", None), P("tgt")),
        out_specs=(P(("tgt", "src"), None), P()),
        check_vma=False,
    )
```

```python
import functools
import math

import jax
import jax.numpy as jnp
from jax import lax
from jax.experimental import pallas as pl
from jax.experimental.pallas import tpu as pltpu
from jax.sharding import PartitionSpec as P

LANES = 128
TURNS = 1.5 / (2.0 * math.pi)
ROUNDER = 12582912.0
SIN_TERMS = (1.570796322, -0.6459634782, 0.07968022286, -0.004602163105)
COS_TERMS = (0.9999999724, -1.233697011, 0.2535986077, -0.02040825547)


def horner(terms, point):
    total = terms[-1]
    for term in terms[-2::-1]:
        total = total * point + term
    return total


def wave_step(tx, ty, sx, sy):
    delta_x = tx - sx
    delta_y = ty - sy
    squared = delta_x * delta_x + delta_y * delta_y + 0.25
    inverse = lax.rsqrt(squared)
    radius = squared * inverse
    radius = radius + (0.5 * inverse) * (squared - radius * radius)
    turns = radius * TURNS
    part = turns - ((turns + ROUNDER) - ROUNDER)
    point = part * part
    sine = horner(SIN_TERMS, point) * part
    cosine = horner(COS_TERMS, point)
    for _ in range(2):
        doubled = sine + sine
        sine, cosine = doubled * cosine, 1.0 - doubled * sine
    decay = jnp.exp2((-0.005 * math.log2(math.e)) * radius)
    return inverse, decay * cosine, decay * sine


def spread_rows(row):
    return jnp.transpose(jnp.broadcast_to(row, (LANES, LANES)))


def pick_coefficients(coef, bodies):
    count = coef.shape[1]
    one_hot = (
        lax.broadcasted_iota(jnp.int32, (count, bodies.shape[1]), 0) == bodies
    ).astype(jnp.float32).astype(jnp.bfloat16)
    picked = None
    rest = coef
    for _ in range(3):
        part = rest.astype(jnp.bfloat16)
        rest = rest - part.astype(jnp.float32)
        term = jnp.dot(part, one_hot, preferred_element_type=jnp.float32)
        picked = term if picked is None else picked + term
    return picked


def remote(source, target, send_sem, recv_sem, axis, peer):
    return pltpu.make_async_remote_copy(
        src_ref=source,
        dst_ref=target,
        send_sem=send_sem,
        recv_sem=recv_sem,
        device_id={axis: peer},
        device_id_type=pl.DeviceIdType.MESH,
    )


def guarded(condition, needed, action):
    if needed:
        pl.when(condition)(action)
    else:
        action()


def sketch_kernel(
    row_block, width, n_src, n_tgt, scale,
    txy_in, sxy_in, body_in, coef_in, probe_in, weight_in, stacked_out, gram_out,
    txy, sxy, body, coef, probe, weight, spread, picked, sums, landed,
    gram_mine, gram_landed, piece_mine, piece_landed, gram_full,
    in_sem, row_send, row_recv, gram_send, gram_recv, tgt_send, tgt_recv, all_send, all_recv,
):
    src_me = lax.axis_index("src")
    tgt_me = lax.axis_index("tgt")
    src_peers = [lax.rem(src_me + offset, n_src) for offset in range(1, n_src)]
    tgt_peers = [lax.rem(tgt_me + offset, n_tgt) for offset in range(1, n_tgt)]
    loads = [
        pltpu.make_async_copy(start, end, in_sem.at[index])
        for index, (start, end) in enumerate(
            ((txy_in, txy), (sxy_in, sxy), (body_in, body), (coef_in, coef),
             (weight_in, weight), (probe_in, probe))
        )
    ]
    for load in loads:
        load.start()
    barrier = pltpu.get_barrier_semaphore()
    for axis, peers in (("src", src_peers), ("tgt", tgt_peers)):
        for peer in peers:
            pl.semaphore_signal(
                barrier, inc=1, device_id={axis: peer}, device_id_type=pl.DeviceIdType.MESH
            )

    rows = txy.shape[1]
    sources = sxy.shape[1]
    terms = coef.shape[0] // 2
    blocks = sources // width
    own = rows // n_src
    chunks = rows // row_block
    owners_in = row_block // own
    rank_width = probe.shape[1]
    piece = piece_mine.shape[0]
    owners = rank_width // piece

    loads[0].wait()
    loads[4].wait()
    for axis in range(3):
        for start in range(0, rows, LANES):
            at = slice(start, start + LANES)
            row = weight[0:1, at] if axis == 2 else txy[axis : axis + 1, at]
            spread[axis, at, :] = spread_rows(row)

    def pick(block, carry):
        at = pl.ds(pl.multiple_of(block * width, width), width)
        picked[:, at] = pick_coefficients(coef[...], body[:, at])
        return carry

    loads[2].wait()
    loads[3].wait()
    lax.fori_loop(0, blocks, pick, 0, unroll=True)
    loads[1].wait()
    loads[5].wait()

    def half(row_at, start):
        at = pl.ds(pl.multiple_of(start, LANES), LANES)
        inverse, step_re, step_im = wave_step(
            spread[0, row_at, :], spread[1, row_at, :], sxy[0:1, at], sxy[1:2, at]
        )

        def term(index):
            return picked[index : index + 1, at]

        total_re, total_im = term(terms - 1), term(2 * terms - 1)
        for degree in range(terms - 2, -1, -1):
            total_re, total_im = (
                (total_re * step_re - total_im * step_im) + term(degree),
                (total_re * step_im + total_im * step_re) + term(terms + degree),
            )
        series_re = total_re * step_re - total_im * step_im
        series_im = total_re * step_im + total_im * step_re
        return (inverse + series_re).astype(jnp.bfloat16), series_im.astype(jnp.bfloat16)

    def tile(row_at, block):
        halves = [half(row_at, block * width + start) for start in range(0, width, LANES)]
        return jnp.concatenate(
            [jnp.concatenate([h[0] for h in halves], axis=1),
             jnp.concatenate([h[1] for h in halves], axis=1)], axis=0)

    def product(held, block):
        at = pl.ds(pl.multiple_of(block * width, width), width)
        return jnp.dot(held, probe[at, :], preferred_element_type=jnp.float32)

    def owned(owner):
        return sums.at[pl.ds(pl.multiple_of(owner * own, own), own), :]

    def chunk(turn, carry):
        index = lax.rem(turn + 1 + src_me // owners_in, chunks)
        row_at = pl.ds(pl.multiple_of(index * row_block, row_block), row_block)

        def step(block, state):
            held, total = state
            total = total + product(held, block - 1)
            return tile(row_at, block), total

        zero = jnp.zeros((2 * row_block, LANES), jnp.float32)
        held, total = lax.fori_loop(1, blocks, step, (tile(row_at, 0), zero))
        total = total + product(held, blocks - 1)
        sums[row_at, :LANES] = total[:row_block]
        sums[row_at, LANES:] = total[row_block:]

        @pl.when(turn == 0)
        def _():
            pl.semaphore_wait(barrier, len(src_peers) + len(tgt_peers))

        for inner in range(owners_in):
            owner = index * owners_in + inner

            @pl.when(owner != src_me)
            def _():
                remote(owned(owner), landed.at[src_me], row_send.at[owner], row_recv.at[src_me],
                       "src", owner).start()

        return carry

    lax.fori_loop(0, chunks, chunk, 0)

    own_at = pl.ds(pl.multiple_of(src_me * own, own), own)
    landed[src_me] = sums[own_at, :]
    for peer in src_peers:
        remote(owned(peer), landed.at[peer], row_send.at[peer], row_recv.at[peer],
               "src", peer).wait()
    total = landed[0]
    for sender in range(1, n_src):
        total = total + landed[sender]
    own_weight = spread[2, own_at, :]
    stacked = jnp.concatenate(
        [total[:, :rank_width] * own_weight, total[:, rank_width:] * own_weight], axis=0)
    gram_mine[...] = lax.dot_general(
        stacked, stacked, (((0,), (0,)), ((), ())),
        precision=lax.Precision.HIGHEST, preferred_element_type=jnp.float32)

    def part_of(ref, owner):
        return ref.at[pl.ds(pl.multiple_of(owner * piece, piece), piece), :]

    some_idle = owners < n_src
    mine = src_me < owners
    for peer in src_peers:
        guarded(peer < owners, some_idle, lambda peer=peer: remote(
            part_of(gram_mine, peer), gram_landed.at[src_me], gram_send.at[peer],
            gram_recv.at[src_me], "src", peer).start())

    def merge():
        at = pl.ds(pl.multiple_of(src_me * piece, piece), piece)
        gram_landed[src_me] = gram_mine[at, :]
        for peer in src_peers:
            remote(part_of(gram_mine, src_me), gram_landed.at[peer], gram_send.at[peer],
                   gram_recv.at[peer], "src", peer).wait_recv()
        merged = gram_landed[0]
        for sender in range(1, n_src):
            merged = merged + gram_landed[sender]
        piece_mine[...] = merged
        copies = [remote(piece_mine, piece_landed.at[tgt_me], tgt_send.at[peer],
                         tgt_recv.at[tgt_me], "tgt", peer) for peer in tgt_peers]
        for copy in copies:
            copy.start()
        piece_landed[tgt_me] = merged
        for peer in tgt_peers:
            remote(piece_mine, piece_landed.at[peer], tgt_send.at[peer],
                   tgt_recv.at[peer], "tgt", peer).wait_recv()
        whole = piece_landed[0]
        for sender in range(1, n_tgt):
            whole = whole + piece_landed[sender]
        gram_full[at, :] = whole * scale
        sends = [remote(part_of(gram_full, src_me), part_of(gram_full, src_me),
                        all_send.at[peer], all_recv.at[src_me], "src", peer)
                 for peer in src_peers]
        for copy in sends:
            copy.start()
        for copy in copies + sends:
            copy.wait_send()

    stacked_out[...] = stacked
    guarded(mine, some_idle, merge)
    for peer in src_peers:
        guarded(peer < owners, some_idle, lambda peer=peer: remote(
            part_of(gram_mine, peer), part_of(gram_full, peer), gram_send.at[peer],
            all_recv.at[peer], "src", peer).wait())
    gram_out[...] = gram_full[...]


def sketch(target_xy, source_xy, body_of, series_coef, probe_matrix, row_weight):
    rows = target_xy.shape[1]
    sources, rank_width = probe_matrix.shape
    n_src = lax.axis_size("src")
    n_tgt = lax.axis_size("tgt")
    own = rows // n_src
    table = series_coef.reshape(-1, series_coef.shape[2])
    inputs = (target_xy, source_xy, body_of[None, :], table, probe_matrix, row_weight[None, :])
    piece = max(8, rank_width // n_src)
    dma = pltpu.SemaphoreType.DMA
    held = [pltpu.VMEM(inputs[i].shape, inputs[i].dtype) for i in range(6)]
    scale = 1.0 / (2.0 * rows * n_tgt)
    return pl.pallas_call(
        functools.partial(sketch_kernel, max(own, math.gcd(rows, 64)), 4 * LANES, n_src, n_tgt, scale),
        out_shape=(
            jax.ShapeDtypeStruct((2 * own, rank_width), jnp.float32),
            jax.ShapeDtypeStruct((rank_width, rank_width), jnp.float32),
        ),
        in_specs=[pl.BlockSpec(memory_space=pl.ANY)] * 6,
        out_specs=[pl.BlockSpec(memory_space=pltpu.VMEM)] * 2,
        scratch_shapes=held + [
            pltpu.VMEM((3, rows, LANES), jnp.float32),
            pltpu.VMEM((table.shape[0], sources), jnp.float32),
            pltpu.VMEM((rows, 2 * rank_width), jnp.float32),
            pltpu.VMEM((n_src, own, 2 * rank_width), jnp.float32),
            pltpu.VMEM((rank_width, rank_width), jnp.float32),
            pltpu.VMEM((n_src, piece, rank_width), jnp.float32),
            pltpu.VMEM((piece, rank_width), jnp.float32),
            pltpu.VMEM((n_tgt, piece, rank_width), jnp.float32),
            pltpu.VMEM((rank_width, rank_width), jnp.float32),
            dma((6,)), dma((n_src,)), dma((n_src,)), dma((n_src,)), dma((n_src,)),
            dma((n_tgt,)), dma((n_tgt,)), dma((n_src,)), dma((n_src,)),
        ],
        compiler_params=pltpu.CompilerParams(
            collective_id=0, has_side_effects=True, vmem_limit_bytes=60 * 1024 * 1024
        ),
        name="sketch",
    )(*inputs)


def factor_kernel(own, stacked, gram, basis, factor, work, inverse):
    size = gram.shape[0]
    rows_at = lax.broadcasted_iota(jnp.int32, (size, size), 0)
    columns_at = lax.broadcasted_iota(jnp.int32, (size, size), 1)
    work[:, :size] = gram[...]
    work[:, size:] = jnp.where(rows_at == columns_at, 1.0, 0.0)
    depth = 32
    sub = lax.broadcasted_iota(jnp.int32, (depth, size), 0)

    def row_of(block, index):
        return jnp.broadcast_to(block[index : index + 1, :], (depth, size))

    for start in range(0, size, depth):
        end = start + depth
        left = work[start:end, :size]
        right = work[start:end, size:]
        columns = [
            jnp.broadcast_to(left[:, start + c : start + c + 1], (depth, size))
            for c in range(depth)
        ]
        pivots = None
        for k in range(depth):
            pivot = row_of(columns[k], k)
            pivots = pivot if pivots is None else jnp.where(sub >= k, pivot, pivots)
            if k == depth - 1:
                break
            ratio = jnp.where(sub > k, columns[k], 0.0) * (1.0 / pivot)
            for c in range(k + 1, depth):
                columns[c] = columns[c] - ratio * row_of(columns[c], k)
            left = left - ratio * row_of(left, k)
            right = right - ratio * row_of(right, k)
        gain = 1.0 / jnp.sqrt(pivots)
        left = left * gain
        right = right * gain
        left = jnp.where(columns_at[:depth] >= start + sub, left, 0.0)
        factor[start:end, :] = left
        inverse[start:end, :] = right
        if end < size:
            both = jnp.concatenate([left, right], axis=1)
            work[end:, :] = work[end:, :] - lax.dot_general(
                left[:, end:], both, (((0,), (0,)), ((), ())),
                precision=lax.Precision.HIGHEST, preferred_element_type=jnp.float32)
    result = lax.dot_general(
        stacked[...], inverse[...], (((1,), (1,)), ((), ())),
        precision=lax.Precision.HIGHEST, preferred_element_type=jnp.float32)
    basis[:, :size] = result[:own]
    basis[:, size:] = result[own:]


def orthonormalize(stacked, gram):
    size = gram.shape[0]
    own = stacked.shape[0] // 2
    return pl.pallas_call(
        functools.partial(factor_kernel, own),
        out_shape=(
            jax.ShapeDtypeStruct((own, 2 * size), jnp.float32),
            jax.ShapeDtypeStruct((size, size), jnp.float32),
        ),
        in_specs=[pl.BlockSpec(memory_space=pltpu.VMEM)] * 2,
        out_specs=[pl.BlockSpec(memory_space=pltpu.VMEM)] * 2,
        scratch_shapes=[
            pltpu.VMEM((size, 2 * size), jnp.float32),
            pltpu.VMEM((size, size), jnp.float32),
        ],
        name="orthonormalize",
    )(stacked, gram)


def per_device(*arguments):
    return orthonormalize(*sketch(*arguments))


def solution(mesh):
    return jax.shard_map(
        per_device,
        mesh=mesh,
        in_specs=(P(None, "tgt"), P(None, "src"), P("src"), P(), P("src", None), P("tgt")),
        out_specs=(P(("tgt", "src"), None), P()),
        check_vma=False,
    )
```
